32 devices in a mesh: section: 8 (over y, x, core), expert: 4 (over z).
Axes of the slice: x: 2, y: 2, z: 4, core: 2. Of those that a mesh axis runs over, the one named last changes fastest.
Arguments:
- act_rows: bfloat16 [8, 512, 2048], P('section', 'expert'), may hold values from -6 to 6
- cot_rows: bfloat16 [8, 512, 2048], P('section', 'expert'), may hold values from -2.390625 to 2.390625
- expert_ids: int32 [8, 512, 1], P('section', 'expert'), may hold values from 0 to 3; in each aligned block of 128 rows (0 to 127, 128 to 255, ..., all dimensions but the last counted through in order) at most 64 rows name the same one
- w_gate: bfloat16 [8, 4, 2048, 128], P('section', 'expert'), may hold values from -0.125 to 0.125
- w_up: bfloat16 [8, 4, 2048, 128], P('section', 'expert'), may hold values from -0.125 to 0.125
- w_down: bfloat16 [8, 4, 128, 2048], P('section', 'expert'), may hold values from -0.375 to 0.375
Outputs:
- act_grad: bfloat16 [8, 512, 2048], P('section', 'expert')
- gate_grad: bfloat16 [8, 4, 2048, 128], P('section', 'expert')
- up_grad: bfloat16 [8, 4, 2048, 128], P('section', 'expert')
- down_grad: bfloat16 [8, 4, 128, 2048], P('section', 'expert')
The draws below stay inside these ranges and needn't reach their ends.
Inputs may be any that keep to these rules, and one draw needn't show every extreme that they name: `expert_ids`: within the 128 rows of one device no expert is named by more than 64 rows, a bound that some block reaches; every expert serves rows somewhere.
All inputs are finite; a program needn't handle non-finite values.
Results may differ from the reference program's by a relative error of at most 0.0049.
Values may be sent and summed in bfloat16 or wider, within the bound.
A program may use at most 64 MiB of HBM per device.

```python
import math
import jax
import jax.numpy as jnp
import numpy as np
from jax import lax

D = 2048
FF = 256
ROWS_DEV = 128
FH = 128
CAP = 64
ROWS = 512
HALF = 4
N_SECTION = 8
N_EXPERT = 4


def level_of(own_key, shape, split, smallest, top_value):
    factor_of = 1.0
    for dim, parts in split:
        draws = jax.random.uniform(jax.random.fold_in(jax.random.fold_in(own_key, 6), dim), (parts,), jnp.float32, smallest / len(split), top_value / len(split))
        factor_of = factor_of * jnp.repeat(jnp.exp(draws), shape[dim] // parts).reshape((-1,) + (1,) * (len(shape) - 1 - dim))
    return factor_of


def routed_block(own_key, own, number, rows, count, top, reach, lean):
    ranking = jax.random.permutation(own_key, count)
    heavy_load, usual = portions_of(count, rows * top, reach, lean, True), portions_of(count, rows * top, reach, lean, False)
    places = jnp.arange(count)

    def named(sizes, offset_by):
        used = int((sizes > 0).sum())
        fixed = max(1, used // 4)
        passed = fixed + (places - fixed + offset_by * (used - fixed)) % max(1, count - fixed)
        return jnp.zeros((count,), jnp.int32).at[ranking[jnp.where(places < fixed, places, passed)]].set(jnp.asarray(sizes, jnp.int32))

    sizes = jnp.where(number % 4 == 0, named(heavy_load, number // 4), named(usual, number - number // 4 - 1))
    mixed = jax.random.permutation(jax.random.fold_in(own, 3), count)
    giver, taker = mixed[0:count // 2 * 2:2], mixed[1:count // 2 * 2:2]
    room = jnp.minimum(sizes[giver] - 1, reach - sizes[taker]) // 2
    room = jnp.where((giver == ranking[0]) | (taker == ranking[0]) | (sizes[taker] == 0), 0, jnp.maximum(room, 0))
    passed = jax.random.randint(jax.random.fold_in(own, 4), (count // 2,), 0, 1 << 20) % (room + 1)
    sizes = sizes.at[giver].add(-passed).at[taker].add(passed)
    members = jnp.searchsorted(jnp.cumsum(sizes), jnp.arange(rows * top), side="right").astype(jnp.int32)
    table = members.reshape(top, rows).T
    table = table[jax.random.permutation(jax.random.fold_in(own, 1), rows)]
    offset_by = jax.random.randint(jax.random.fold_in(own, 2), (rows, 1), 0, top)
    return jnp.take_along_axis(table, (jnp.arange(top)[None, :] + offset_by) % top, axis=1)


def portions_of(count, total, reach, slope, full):
    weights = [(1 << 20) // math.isqrt(rank ** slope) + 1 for rank in range(1, count + 1)]
    largest = reach if full else min(reach, max(-(-total // count), total * weights[0] // sum(weights)))
    least = 1 if total - largest >= count - 1 else 0
    given, rest = [largest] + [least] * (count - 1), total - largest - least * (count - 1)
    while rest > 0:
        candidates = [i for i in range(1, count) if given[i] < largest] or [i for i in range(1, count) if given[i] < reach]
        whole, left = sum([weights[i] for i in candidates]), rest
        for i in candidates:
            more = min(reach - given[i], max(1, left * weights[i] // whole), rest)
            given[i] = given[i] + more
            rest = rest - more
    return np.array(given)


def noise(rng, dims, width, most, split=(), kind=jnp.bfloat16):
    factor_of = level_of(rng, dims, split, -0.22, 0.18) if split else 1.0
    result = jax.random.normal(rng, dims, jnp.float32) * width * factor_of
    return jnp.minimum(jnp.maximum(result, -most), most).astype(kind)


def setup_inputs(seed: int = 0) -> dict:
    key_of = jax.random.split(jax.random.key(seed), 7)
    act_rows = noise(key_of[0], (N_SECTION, ROWS, D), 1.0, 6.0, ((0, 8), (1, 4)))
    cot_rows = noise(key_of[1], (N_SECTION, ROWS, D), 0.4, 2.390625, ((0, 8), (1, 4)))
    expert_ids_keys = jax.random.split(jax.random.fold_in(key_of[2], 1), N_SECTION * ROWS // ROWS_DEV)
    expert_ids_turns = jax.random.permutation(jax.random.fold_in(key_of[2], 3), N_SECTION * ROWS // ROWS_DEV)
    expert_ids = jax.vmap(lambda own, number: routed_block(jax.random.fold_in(key_of[2], 2), own, number, ROWS_DEV, N_EXPERT, 1, CAP, 1))(expert_ids_keys, expert_ids_turns).reshape((N_SECTION, ROWS, 1))
    w_gate = noise(key_of[3], (N_SECTION, N_EXPERT, D, FH), D ** -0.5, 0.125, ((0, 8), (1, 4)))
    w_up = noise(key_of[4], (N_SECTION, N_EXPERT, D, FH), D ** -0.5, 0.125, ((0, 8), (1, 4)))
    w_down = noise(key_of[5], (N_SECTION, N_EXPERT, FH, D), FF ** -0.5, 0.375, ((0, 8), (1, 4)))
    return {"act_rows": act_rows, "cot_rows": cot_rows, "expert_ids": expert_ids, "w_gate": w_gate, "w_up": w_up, "w_down": w_down}


def expert_pass(act_buf, cot_buf, gate_full, up_full, down_full):
    gate_pre = jnp.dot(act_buf, gate_full, preferred_element_type=jnp.float32)
    up_pre = jnp.dot(act_buf, up_full, preferred_element_type=jnp.float32)
    sigma = jax.nn.sigmoid(gate_pre)
    activ = gate_pre * sigma
    hidden = (activ * up_pre).astype(jnp.bfloat16)
    hidden_grad = jnp.dot(cot_buf, down_full.T, preferred_element_type=jnp.float32)
    gate_delta = (hidden_grad * up_pre * sigma * (1.0 + gate_pre * (1.0 - sigma))).astype(jnp.bfloat16)
    up_delta = (hidden_grad * activ).astype(jnp.bfloat16)
    act_back = (jnp.dot(gate_delta, gate_full.T, preferred_element_type=jnp.float32)
                + jnp.dot(up_delta, up_full.T, preferred_element_type=jnp.float32)).astype(jnp.bfloat16)
    gate_sum = jnp.dot(act_buf.T, gate_delta, preferred_element_type=jnp.float32)
    up_sum = jnp.dot(act_buf.T, up_delta, preferred_element_type=jnp.float32)
    down_sum = jnp.dot(hidden.T, cot_buf, preferred_element_type=jnp.float32)
    return act_back, gate_sum, up_sum, down_sum


def section_pass(act_section, cot_section, route_ids, gate_full, up_full, down_full):
    blocks = route_ids.reshape(N_EXPERT, ROWS_DEV)
    onehot = (blocks[:, :, None] == jnp.arange(N_EXPERT, dtype=jnp.int32)[None, None, :]).astype(jnp.int32)
    ranks = jnp.cumsum(onehot, axis=1) - onehot
    slots = jnp.sum(ranks * onehot, axis=2)
    source = jnp.arange(N_EXPERT, dtype=jnp.int32)[:, None]
    places = (blocks * (N_EXPERT * CAP) + source * CAP + slots).reshape(-1).astype(jnp.int32)
    total = N_EXPERT * N_EXPERT * CAP
    act_buf = jnp.zeros((total, D), act_section.dtype).at[places].set(act_section).reshape(N_EXPERT, N_EXPERT * CAP, D)
    cot_buf = jnp.zeros((total, D), cot_section.dtype).at[places].set(cot_section).reshape(N_EXPERT, N_EXPERT * CAP, D)
    act_back, gate_sum, up_sum, down_sum = lax.map(
        lambda operands: expert_pass(*operands), (act_buf, cot_buf, gate_full, up_full, down_full))
    return act_back.reshape(total, D)[places], gate_sum, up_sum, down_sum


def reference(act_rows, cot_rows, expert_ids, w_gate, w_up, w_down):
    def layer_pass(layer_index):
        low_section = layer_index
        high_section = layer_index + HALF
        gate_full = jnp.concatenate([w_gate[low_section], w_gate[high_section]], axis=2)
        up_full = jnp.concatenate([w_up[low_section], w_up[high_section]], axis=2)
        down_full = jnp.concatenate([w_down[low_section], w_down[high_section]], axis=1)
        first_pass = section_pass(act_rows[low_section], cot_rows[low_section], expert_ids[low_section, :, 0],
                                gate_full, up_full, down_full)
        second_pass = section_pass(act_rows[high_section], cot_rows[high_section], expert_ids[high_section, :, 0],
                                 gate_full, up_full, down_full)
        gate_total = (first_pass[1] + second_pass[1]).astype(jnp.bfloat16)
        up_total = (first_pass[2] + second_pass[2]).astype(jnp.bfloat16)
        down_total = (first_pass[3] + second_pass[3]).astype(jnp.bfloat16)
        return (first_pass[0], second_pass[0],
                gate_total[:, :, :FH], gate_total[:, :, FH:],
                up_total[:, :, :FH], up_total[:, :, FH:],
                down_total[:, :FH, :], down_total[:, FH:, :])

    results = lax.map(layer_pass, jnp.arange(HALF, dtype=jnp.int32))
    act_grad = jnp.concatenate([results[0], results[1]], axis=0)
    gate_grad = jnp.concatenate([results[2], results[3]], axis=0)
    up_grad = jnp.concatenate([results[4], results[5]], axis=0)
    down_grad = jnp.concatenate([results[6], results[7]], axis=0)
    return act_grad, gate_grad, up_grad, down_grad
```

```python
import functools
import math

import jax
import jax.numpy as jnp
from jax import lax
from jax.experimental import pallas as pl
from jax.experimental.pallas import tpu as pltpu
from jax.sharding import PartitionSpec as P

MESH = pl.DeviceIdType.MESH
F32 = jnp.float32
BF16 = jnp.bfloat16


def dot(a, b, a_dim, b_dim):
    return lax.dot_general(a, b, (((a_dim,), (b_dim,)), ((), ())), preferred_element_type=F32)


def partner_of(own, k, count):
    other = own
    bit = 1
    while bit < count:
        if k & bit:
            other = other + bit - 2 * bit * ((own // bit) % 2)
        bit *= 2
    return other


def kernel(
    n_experts, n_groups, cap,
    act_ref, cot_ref, ids_ref, wg_ref, wu_ref, wd_ref,
    out_ref, gate_ref, up_ref, down_ref,
    w_cat, send_a, send_c, rows_a, rows_c, delta, hidden, own_back, mate_out, mate_in, ret_out, ret_in,
    zs, zr, ys, yr, bs, br, rs, rr,
):
    n_rows, width = act_ref.shape
    units = wg_ref.shape[1]
    slots = n_experts * cap
    group = slots // n_groups
    per_group = n_experts // n_groups
    half = lax.axis_size("section") // 2
    section = lax.axis_index("section")
    own = lax.axis_index("expert")
    mate = {"section": (section + half) % (2 * half)}
    partners = [{"expert": partner_of(own, k, n_experts)} for k in range(n_experts)]

    barrier = pltpu.get_barrier_semaphore()
    for peer in partners[1:] + [mate]:
        pl.semaphore_signal(barrier, inc=1, device_id=peer, device_id_type=MESH)

    def remote(src, dst, send_sem, recv_sem, peer):
        return pltpu.make_async_remote_copy(
            src_ref=src, dst_ref=dst, send_sem=send_sem, recv_sem=recv_sem, device_id=peer, device_id_type=MESH
        )

    def chunk(k):
        return pl.ds(k * cap, cap)

    def rows_of(g, section_part=0):
        return pl.ds(section_part * slots + g * group, group)

    z_copies = [None] + [
        [
            remote(send_a.at[chunk(k)], rows_a.at[chunk(k)], zs.at[0, k], zr.at[0, k], partners[k]),
            remote(send_c.at[chunk(k)], rows_c.at[chunk(k)], zs.at[1, k], zr.at[1, k], partners[k]),
        ]
        for k in range(1, n_experts)
    ]
    y_copies = [
        [
            remote(rows_a.at[rows_of(g)], rows_a.at[rows_of(g, 1)], ys.at[0, g], yr.at[0, g], mate),
            remote(rows_c.at[rows_of(g)], rows_c.at[rows_of(g, 1)], ys.at[1, g], yr.at[1, g], mate),
        ]
        for g in range(n_groups)
    ]
    b_copies = [
        remote(mate_out.at[rows_of(g)], mate_in.at[rows_of(g)], bs.at[g], br.at[g], mate) for g in range(n_groups)
    ]
    r_copies = [None] + [
        remote(ret_out.at[chunk(k)], ret_in.at[chunk(k)], rs.at[k], rr.at[k], partners[k])
        for k in range(1, n_experts)
    ]

    rel = ids_ref[...] ^ own
    onehot = (lax.broadcasted_iota(jnp.int32, (n_rows, 128), 1) == rel).astype(F32)
    below = (
        lax.broadcasted_iota(jnp.int32, (n_rows, n_rows), 0) > lax.broadcasted_iota(jnp.int32, (n_rows, n_rows), 1)
    ).astype(F32)
    ranks = dot(below.astype(BF16), onehot.astype(BF16), 1, 0)
    place = rel * cap + jnp.sum(ranks * onehot, axis=1, keepdims=True).astype(jnp.int32)
    spread = (lax.broadcasted_iota(jnp.int32, (n_rows, slots), 1) == place).astype(F32).astype(BF16)

    packed = dot(spread, act_ref[...], 0, 0).astype(BF16)
    send_a[...] = packed
    rows_a[chunk(0)] = packed[:cap]
    packed = dot(spread, cot_ref[...], 0, 0).astype(BF16)
    send_c[...] = packed
    rows_c[chunk(0)] = packed[:cap]

    pl.semaphore_wait(barrier, n_experts)
    order = [0, 1, 3, 2] if n_groups == 4 else list(range(n_groups))
    for g in order:
        for k in range(g * per_group, (g + 1) * per_group):
            if k > 0:
                for copy in z_copies[k]:
                    copy.start()

    w_cat[:, :units] = wg_ref[...]
    w_cat[:, units:] = wu_ref[...]

    def arrive(g):
        for part in range(2):
            for k in range(g * per_group, (g + 1) * per_group):
                if k > 0:
                    z_copies[k][part].wait_recv()
            y_copies[g][part].start()

    def work(rows):
        pre = dot(rows_a[rows], w_cat[...], 1, 0)
        gate_pre, up_pre = pre[:, :units], pre[:, units:]
        hidden_grad = dot(rows_c[rows], wd_ref[...], 1, 1)
        sigma = 1.0 / (1.0 + jnp.exp(-gate_pre))
        activ = gate_pre * sigma
        hidden[rows] = (activ * up_pre).astype(BF16)
        delta[rows, :units] = (hidden_grad * up_pre * sigma * (1.0 + gate_pre * (1.0 - sigma))).astype(BF16)
        delta[rows, units:] = (hidden_grad * activ).astype(BF16)
        return dot(delta[rows], w_cat[...], 1, 1)

    def own_work(g):
        own_back[rows_of(g)] = work(rows_of(g))

    def mate_work(g):
        for copy in y_copies[g]:
            copy.wait_recv()
        mate_out[rows_of(g)] = work(rows_of(g, 1)).astype(BF16)
        b_copies[g].start()

    def give_back(g):
        b_copies[g].wait_recv()
        total = (own_back[rows_of(g)] + mate_in[rows_of(g)].astype(F32)).astype(BF16)
        ret_out[rows_of(g)] = total
        for k in range(g * per_group, (g + 1) * per_group):
            if k > 0:
                r_copies[k].start()
            else:
                ret_in[chunk(0)] = total[:cap]

    for i in range(n_groups + 2):
        if i < n_groups:
            arrive(order[i])
            own_work(order[i])
        if 1 <= i <= n_groups:
            mate_work(order[i - 1])
        if i >= 2:
            give_back(order[i - 2])

    tile = 256
    for at in range(0, width, tile):
        cols = pl.ds(at, tile)
        grads = dot(rows_a[:, cols], delta[...], 0, 0)
        gate_ref[cols] = grads[:, :units].astype(BF16)
        up_ref[cols] = grads[:, units:].astype(BF16)
    down_ref[...] = dot(hidden[...], rows_c[...], 0, 0).astype(BF16)

    for copy in r_copies[1:]:
        copy.wait_recv()
    out_ref[...] = dot(spread, ret_in[...], 1, 0).astype(BF16)

    for k in range(1, n_experts):
        for copy in z_copies[k]:
            copy.wait_send()
        r_copies[k].wait_send()
    for g in range(n_groups):
        for copy in y_copies[g]:
            copy.wait_send()
        b_copies[g].wait_send()


def per_device(act_rows, cot_rows, expert_ids, w_gate, w_up, w_down):
    n_experts = lax.axis_size("expert")
    n_rows, width = act_rows.shape[1:]
    units = w_gate.shape[3]
    cap = 2 * n_rows // n_experts
    slots = n_experts * cap
    n_groups = math.gcd(n_experts, 4)
    dma = pltpu.SemaphoreType.DMA
    vmem = pl.BlockSpec(memory_space=pltpu.VMEM)
    outs = pl.pallas_call(
        functools.partial(kernel, n_experts, n_groups, cap),
        out_shape=(
            jax.ShapeDtypeStruct((n_rows, width), BF16),
            jax.ShapeDtypeStruct((width, units), BF16),
            jax.ShapeDtypeStruct((width, units), BF16),
            jax.ShapeDtypeStruct((units, width), BF16),
        ),
        in_specs=[vmem] * 6,
        out_specs=(vmem,) * 4,
        scratch_shapes=[
            pltpu.VMEM((width, 2 * units), BF16),
            pltpu.VMEM((slots, width), BF16),
            pltpu.VMEM((slots, width), BF16),
            pltpu.VMEM((2 * slots, width), BF16),
            pltpu.VMEM((2 * slots, width), BF16),
            pltpu.VMEM((2 * slots, 2 * units), BF16),
            pltpu.VMEM((2 * slots, units), BF16),
            pltpu.VMEM((slots, width), F32),
            pltpu.VMEM((slots, width), BF16),
            pltpu.VMEM((slots, width), BF16),
            pltpu.VMEM((slots, width), BF16),
            pltpu.VMEM((slots, width), BF16),
            dma((2, n_experts)),
            dma((2, n_experts)),
            dma((2, n_groups)),
            dma((2, n_groups)),
            dma((n_groups,)),
            dma((n_groups,)),
            dma((n_experts,)),
            dma((n_experts,)),
        ],
        compiler_params=pltpu.CompilerParams(
            collective_id=0, has_side_effects=True, vmem_limit_bytes=48 * 1024 * 1024
        ),
        cost_estimate=pl.CostEstimate(
            flops=32 * slots * width * units, bytes_accessed=9 * n_rows * width * 2, transcendentals=2 * slots * units
        ),
    )(act_rows[0], cot_rows[0], expert_ids[0], w_gate[0, 0], w_up[0, 0], w_down[0, 0])
    return (outs[0][None], outs[1][None, None], outs[2][None, None], outs[3][None, None])


def solution(mesh):
    rows = P("section", "expert", None)
    weights = P("section", "expert", None, None)
    return jax.shard_map(
        per_device,
        mesh=mesh,
        in_specs=(rows, rows, rows, weights, weights, weights),
        out_specs=(rows, weights, weights, weights),
        check_vma=False,
    )
```

```python
import functools

import jax
import jax.numpy as jnp
from jax import lax
from jax.experimental import pallas as pl
from jax.experimental.pallas import tpu as pltpu
from jax.sharding import PartitionSpec as P

MESH = pl.DeviceIdType.MESH
F32 = jnp.float32
BF16 = jnp.bfloat16


def dot(a, b, a_dim, b_dim):
    return lax.dot_general(a, b, (((a_dim,), (b_dim,)), ((), ())), preferred_element_type=F32)


def partner_of(own, k, count):
    other = own
    bit = 1
    while bit < count:
        if k & bit:
            other = other + bit - 2 * bit * ((own // bit) % 2)
        bit *= 2
    return other


def kernel(
    n_experts, n_groups, cap,
    act_ref, cot_ref, ids_ref, wg_ref, wu_ref, wd_ref,
    out_hbm, gate_hbm, up_hbm, down_hbm,
    out_ref, gate_ref, up_ref, down_ref, act, cot, w_cat, wd, send, rows, delta, hidden, own_back, mate_out, mate_in, ret_out, ret_in,
    loads, stores, zs, zr, ys, yr, bs, br, rs, rr,
):
    n_rows, width = act_ref.shape
    units = wg_ref.shape[1]
    slots = n_experts * cap
    group = slots // n_groups
    piece = min(cap, group)
    n_pieces = slots // piece
    per_group = n_pieces // n_groups
    half = lax.axis_size("section") // 2
    section = lax.axis_index("section")
    own = lax.axis_index("expert")
    mate = {"section": (section + half) % (2 * half)}
    partners = [{"expert": partner_of(own, k, n_experts)} for k in range(n_experts)]

    fetch = [
        pltpu.make_async_copy(src, dst, loads.at[i])
        for i, (src, dst) in enumerate(
            [
                (act_ref, act),
                (cot_ref, cot),
                (wg_ref, w_cat.at[:, pl.ds(0, units)]),
                (wu_ref, w_cat.at[:, pl.ds(units, units)]),
                (wd_ref, wd),
            ]
        )
    ]
    for copy in fetch:
        copy.start()

    barrier = pltpu.get_barrier_semaphore()
    for peer in partners[1:] + [mate]:
        pl.semaphore_signal(barrier, inc=1, device_id=peer, device_id_type=MESH)

    def remote(src, dst, send_sem, recv_sem, peer):
        return pltpu.make_async_remote_copy(
            src_ref=src, dst_ref=dst, send_sem=send_sem, recv_sem=recv_sem, device_id=peer, device_id_type=MESH
        )

    def peer_of(p):
        return p * piece // cap

    def piece_rows(p):
        return pl.ds(p * piece, piece)

    def rows_of(g, section_part=0):
        return pl.ds(section_part * slots + g * group, group)

    def pieces(g):
        return [p for p in range(g * per_group, (g + 1) * per_group) if peer_of(p) > 0]

    z_copies = [
        remote(send.at[piece_rows(p)], rows.at[piece_rows(p)], zs.at[p], zr.at[p], partners[peer_of(p)])
        if peer_of(p) > 0 else None
        for p in range(n_pieces)
    ]
    y_copies = [remote(rows.at[rows_of(g)], rows.at[rows_of(g, 1)], ys.at[g], yr.at[g], mate) for g in range(n_groups)]
    b_copies = [
        remote(mate_out.at[rows_of(g)], mate_in.at[rows_of(g)], bs.at[g], br.at[g], mate) for g in range(n_groups)
    ]
    r_copies = [
        remote(ret_out.at[piece_rows(p)], ret_in.at[piece_rows(p)], rs.at[p], rr.at[p], partners[peer_of(p)])
        if peer_of(p) > 0 else None
        for p in range(n_pieces)
    ]

    rel = ids_ref[...] ^ own
    kinds = -(-n_experts // 16) * 16
    onehot = (lax.broadcasted_iota(jnp.int32, (kinds, n_rows), 0) == rel).astype(F32)
    above = (
        lax.broadcasted_iota(jnp.int32, (n_rows, n_rows), 0) < lax.broadcasted_iota(jnp.int32, (n_rows, n_rows), 1)
    ).astype(F32)
    ranks = dot(onehot.astype(BF16), above.astype(BF16), 1, 0)
    place = rel * cap + jnp.sum(ranks * onehot, axis=0, keepdims=True).astype(jnp.int32)
    spread = (lax.broadcasted_iota(jnp.int32, (slots, n_rows), 0) == place).astype(F32).astype(BF16)

    for i, source in enumerate((act, cot)):
        fetch[i].wait()
        packed = dot(spread, source[...], 1, 0).astype(BF16)
        cols = pl.ds(i * width, width)
        send[cap:, cols] = packed[cap:]
        rows[:cap, cols] = packed[:cap]

    order = list(range(n_groups))
    if n_groups == 8:
        order = [0, 1, 2, 3, 6, 7, 4, 5]
    late = order[-2:]

    def send_group(g):
        for p in pieces(g):
            z_copies[p].start()

    def sent_group(g):
        for p in pieces(g):
            z_copies[p].wait_send()

    pl.semaphore_wait(barrier, n_experts)
    for g in order[:-2]:
        send_group(g)

    def arrive(g):
        for p in pieces(g):
            z_copies[p].wait_recv()
        y_copies[g].start()

    def work(at):
        pre = dot(rows[at, :width], w_cat[...], 1, 0)
        gate_pre, up_pre = pre[:, :units], pre[:, units:]
        hidden_grad = dot(rows[at, width:], wd[...], 1, 1)
        sigma = 1.0 / (1.0 + jnp.exp(-gate_pre))
        activ = gate_pre * sigma
        hidden[at] = (activ * up_pre).astype(BF16)
        delta[at, :units] = (hidden_grad * up_pre * sigma * (1.0 + gate_pre * (1.0 - sigma))).astype(BF16)
        delta[at, units:] = (hidden_grad * activ).astype(BF16)
        return dot(delta[at], w_cat[...], 1, 1)

    def own_work(g):
        own_back[rows_of(g)] = work(rows_of(g))

    def mate_work(g):
        y_copies[g].wait_recv()
        mate_out[rows_of(g)] = work(rows_of(g, 1)).astype(BF16)
        b_copies[g].start()

    def give_back(g):
        b_copies[g].wait_recv()
        total = (own_back[rows_of(g)] + mate_in[rows_of(g)].astype(F32)).astype(BF16)
        ret_out[rows_of(g)] = total
        for p in range(g * per_group, (g + 1) * per_group):
            if peer_of(p) > 0:
                r_copies[p].start()
            else:
                ret_in[piece_rows(p)] = total[(p - g * per_group) * piece:(p - g * per_group + 1) * piece]

    for i in range(n_groups + 3):
        if i < n_groups:
            if order[i] == late[0]:
                sent_group(late[0])
                send_group(late[1])
            arrive(order[i])
            if i == n_groups - 3:
                send_group(late[0])
            if i == 0:
                for copy in fetch[2:]:
                    copy.wait()
            own_work(order[i])
        if 1 <= i <= n_groups:
            mate_work(order[i - 1])
        if i >= 3:
            give_back(order[i - 3])

    store = [
        pltpu.make_async_copy(src, dst, stores.at[i])
        for i, (src, dst) in enumerate(
            [(out_ref, out_hbm), (gate_ref, gate_hbm), (up_ref, up_hbm), (down_ref, down_hbm)]
        )
    ]
    tile = 256
    for at in range(0, width, tile):
        cols = pl.ds(at, tile)
        grads = dot(rows[:, cols], delta[...], 0, 0)
        gate_ref[cols] = grads[:, :units].astype(BF16)
        up_ref[cols] = grads[:, units:].astype(BF16)
    down_ref[...] = dot(hidden[...], rows[:, width:], 0, 0).astype(BF16)

    for copy in store[1:]:
        copy.start()

    for g in order:
        for p in pieces(g):
            r_copies[p].wait_recv()
    out_ref[...] = dot(spread, ret_in[...], 0, 0).astype(BF16)
    store[0].start()

    for g in range(n_groups):
        if g != late[0]:
            sent_group(g)
        for p in pieces(g):
            r_copies[p].wait_send()
        y_copies[g].wait_send()
        b_copies[g].wait_send()
    for copy in store:
        copy.wait()


def write_out(*refs):
    count = len(refs) // 2
    sems = refs[-1]
    copies = [pltpu.make_async_copy(refs[i], refs[count + i], sems.at[i]) for i in range(count)]
    for copy in copies:
        copy.start()
    for copy in copies:
        copy.wait()


def per_device(act_rows, cot_rows, expert_ids, w_gate, w_up, w_down):
    n_experts = lax.axis_size("expert")
    n_rows, width = act_rows.shape[1:]
    units = w_gate.shape[3]
    cap = 2 * n_rows // n_experts
    slots = n_experts * cap
    n_groups = slots // 32
    n_pieces = slots // min(cap, 32)
    dma = pltpu.SemaphoreType.DMA
    vmem = pl.BlockSpec(memory_space=pltpu.VMEM)
    hbm = pl.BlockSpec(memory_space=pltpu.HBM)
    shapes = (
        jax.ShapeDtypeStruct((n_rows, width), BF16),
        jax.ShapeDtypeStruct((width, units), BF16),
        jax.ShapeDtypeStruct((width, units), BF16),
        jax.ShapeDtypeStruct((units, width), BF16),
    )
    results = pl.pallas_call(
        functools.partial(kernel, n_experts, n_groups, cap),
        out_shape=shapes,
        in_specs=[hbm, hbm, vmem, hbm, hbm, hbm],
        out_specs=(hbm,) * 4,
        scratch_shapes=[
            pltpu.VMEM((n_rows, width), BF16),
            pltpu.VMEM((width, units), BF16),
            pltpu.VMEM((width, units), BF16),
            pltpu.VMEM((units, width), BF16),
            pltpu.VMEM((n_rows, width), BF16),
            pltpu.VMEM((n_rows, width), BF16),
            pltpu.VMEM((width, 2 * units), BF16),
            pltpu.VMEM((units, width), BF16),
            pltpu.VMEM((slots, 2 * width), BF16),
            pltpu.VMEM((2 * slots, 2 * width), BF16),
            pltpu.VMEM((2 * slots, 2 * units), BF16),
            pltpu.VMEM((2 * slots, units), BF16),
            pltpu.VMEM((slots, width), F32),
            pltpu.VMEM((slots, width), BF16),
            pltpu.VMEM((slots, width), BF16),
            pltpu.VMEM((slots, width), BF16),
            pltpu.VMEM((slots, width), BF16),
            dma((5,)),
            dma((4,)),
            dma((n_pieces,)),
            dma((n_pieces,)),
            dma((n_groups,)),
            dma((n_groups,)),
            dma((n_groups,)),
            dma((n_groups,)),
            dma((n_pieces,)),
            dma((n_pieces,)),
        ],
        compiler_params=pltpu.CompilerParams(
            collective_id=0, has_side_effects=True, vmem_limit_bytes=60 * 1024 * 1024
        ),
        cost_estimate=pl.CostEstimate(
            flops=32 * slots * width * units, bytes_accessed=9 * n_rows * width * 2, transcendentals=2 * slots * units
        ),
    )(act_rows[0], cot_rows[0], expert_ids.reshape(1, n_rows), w_gate[0, 0], w_up[0, 0], w_down[0, 0])
    outs = pl.pallas_call(
        write_out,
        out_shape=shapes,
        in_specs=[hbm] * 4,
        out_specs=(hbm,) * 4,
        scratch_shapes=[dma((4,))],
        cost_estimate=pl.CostEstimate(flops=0, bytes_accessed=16 * width * units, transcendentals=0),
    )(*results)
    return (outs[0][None], outs[1][None, None], outs[2][None, None], outs[3][None, None])


def solution(mesh):
    rows = P("section", "expert", None)
    weights = P("section", "expert", None, None)
    return jax.shard_map(
        per_device,
        mesh=mesh,
        in_specs=(rows, rows, rows, weights, weights, weights),
        out_specs=(rows, weights, weights, weights),
        check_vma=False,
    )
```

```python
import functools

import jax
import jax.numpy as jnp
from jax import lax
from jax.experimental import pallas as pl
from jax.experimental.pallas import tpu as pltpu
from jax.sharding import PartitionSpec as P

MESH = pl.DeviceIdType.MESH
F32 = jnp.float32
BF16 = jnp.bfloat16


def dot(a, b, a_dim, b_dim):
    return lax.dot_general(a, b, (((a_dim,), (b_dim,)), ((), ())), preferred_element_type=F32)


def partner_of(own, k, count):
    other = own
    bit = 1
    while bit < count:
        if k & bit:
            other = other + bit - 2 * bit * ((own // bit) % 2)
        bit *= 2
    return other


def kernel(
    n_experts, n_groups, cap,
    act_ref, cot_ref, ids_ref, wg_ref, wu_ref, wd_ref,
    out_hbm, gate_hbm, up_hbm, down_hbm,
    out_ref, gate_ref, up_ref, down_ref, act, cot, w_cat, wd, send, rows, delta, hidden, own_back, mate_out, mate_in, ret_out, ret_in,
    loads, stores, zs, zr, ys, yr, bs, br, rs, rr,
):
    n_rows, width = act_ref.shape
    units = wg_ref.shape[1]
    slots = n_experts * cap
    group = slots // n_groups
    piece = min(cap, group)
    n_pieces = slots // piece
    per_group = n_pieces // n_groups
    half = lax.axis_size("section") // 2
    section = lax.axis_index("section")
    own = lax.axis_index("expert")
    mate = {"section": (section + half) % (2 * half)}
    partners = [{"expert": partner_of(own, k, n_experts)} for k in range(n_experts)]

    fetch = [
        pltpu.make_async_copy(src, dst, loads.at[i])
        for i, (src, dst) in enumerate(
            [
                (act_ref, act),
                (cot_ref, cot),
                (wg_ref, w_cat.at[:, pl.ds(0, units)]),
                (wu_ref, w_cat.at[:, pl.ds(units, units)]),
                (wd_ref, wd),
            ]
        )
    ]
    for copy in fetch:
        copy.start()

    barrier = pltpu.get_barrier_semaphore()
    for peer in partners[1:] + [mate]:
        pl.semaphore_signal(barrier, inc=1, device_id=peer, device_id_type=MESH)

    def remote(src, dst, send_sem, recv_sem, peer):
        return pltpu.make_async_remote_copy(
            src_ref=src, dst_ref=dst, send_sem=send_sem, recv_sem=recv_sem, device_id=peer, device_id_type=MESH
        )

    def peer_of(p):
        return p * piece // cap

    def piece_rows(p):
        return pl.ds(p * piece, piece)

    def rows_of(g, section_part=0):
        return pl.ds(section_part * slots + g * group, group)

    def pieces(g):
        return [p for p in range(g * per_group, (g + 1) * per_group) if peer_of(p) > 0]

    z_copies = [
        remote(send.at[piece_rows(p)], rows.at[piece_rows(p)], zs.at[p], zr.at[p], partners[peer_of(p)])
        if peer_of(p) > 0 else None
        for p in range(n_pieces)
    ]
    y_copies = [remote(rows.at[rows_of(g)], rows.at[rows_of(g, 1)], ys.at[g], yr.at[g], mate) for g in range(n_groups)]
    b_copies = [
        remote(mate_out.at[rows_of(g)], mate_in.at[rows_of(g)], bs.at[g], br.at[g], mate) for g in range(n_groups)
    ]
    r_copies = [
        remote(ret_out.at[piece_rows(p)], ret_in.at[piece_rows(p)], rs.at[p], rr.at[p], partners[peer_of(p)])
        if peer_of(p) > 0 else None
        for p in range(n_pieces)
    ]

    rel = ids_ref[...] ^ own
    kinds = -(-n_experts // 16) * 16
    onehot = (lax.broadcasted_iota(jnp.int32, (kinds, n_rows), 0) == rel).astype(F32)
    above = (
        lax.broadcasted_iota(jnp.int32, (n_rows, n_rows), 0) < lax.broadcasted_iota(jnp.int32, (n_rows, n_rows), 1)
    ).astype(F32)
    ranks = dot(onehot.astype(BF16), above.astype(BF16), 1, 0)
    place = rel * cap + jnp.sum(ranks * onehot, axis=0, keepdims=True).astype(jnp.int32)
    spread = (lax.broadcasted_iota(jnp.int32, (slots, n_rows), 0) == place).astype(F32).astype(BF16)

    for i, source in enumerate((act, cot)):
        fetch[i].wait()
        packed = dot(spread, source[...], 1, 0).astype(BF16)
        cols = pl.ds(i * width, width)
        send[cap:, cols] = packed[cap:]
        rows[:cap, cols] = packed[:cap]

    order = list(range(n_groups))
    if n_groups == 8:
        order = [0, 1, 2, 3, 6, 7, 4, 5]
    late = order[-2:]

    def send_group(g):
        for p in pieces(g):
            z_copies[p].start()

    def sent_group(g):
        for p in pieces(g):
            z_copies[p].wait_send()

    pl.semaphore_wait(barrier, n_experts)
    held_back = order[4:6] if n_groups == 8 and n_experts == 4 else []
    for g in order[:-2]:
        if g not in held_back:
            send_group(g)
    inner = ((own + 1) // 2) % 2 == 1

    if held_back:
        @pl.when(inner)
        def _():
            for g in held_back:
                send_group(g)

    def arrive(g):
        for p in pieces(g):
            z_copies[p].wait_recv()
        y_copies[g].start()

    def work(at):
        pre = dot(rows[at, :width], w_cat[...], 1, 0)
        gate_pre, up_pre = pre[:, :units], pre[:, units:]
        hidden_grad = dot(rows[at, width:], wd[...], 1, 1)
        sigma = 1.0 / (1.0 + jnp.exp(-gate_pre))
        activ = gate_pre * sigma
        hidden[at] = (activ * up_pre).astype(BF16)
        delta[at, :units] = (hidden_grad * up_pre * sigma * (1.0 + gate_pre * (1.0 - sigma))).astype(BF16)
        delta[at, units:] = (hidden_grad * activ).astype(BF16)
        return dot(delta[at], w_cat[...], 1, 1)

    def own_work(g):
        own_back[rows_of(g)] = work(rows_of(g))

    def mate_work(g):
        y_copies[g].wait_recv()
        mate_out[rows_of(g)] = work(rows_of(g, 1)).astype(BF16)
        b_copies[g].start()

    def give_back(g):
        b_copies[g].wait_recv()
        total = (own_back[rows_of(g)] + mate_in[rows_of(g)].astype(F32)).astype(BF16)
        ret_out[rows_of(g)] = total
        for p in range(g * per_group, (g + 1) * per_group):
            if peer_of(p) > 0:
                r_copies[p].start()
            else:
                ret_in[piece_rows(p)] = total[(p - g * per_group) * piece:(p - g * per_group + 1) * piece]

    for i in range(n_groups + 3):
        if i < n_groups:
            if order[i] == late[0]:
                sent_group(late[0])
                send_group(late[1])
            arrive(order[i])
            if i == 3 and held_back:
                @pl.when(jnp.logical_not(inner))
                def _():
                    for g in held_back:
                        send_group(g)
            if i == n_groups - 3:
                send_group(late[0])
            if i == 0:
                for copy in fetch[2:]:
                    copy.wait()
            own_work(order[i])
        if 1 <= i <= n_groups:
            mate_work(order[i - 1])
        if i >= 3:
            give_back(order[i - 3])

    store = [
        pltpu.make_async_copy(src, dst, stores.at[i])
        for i, (src, dst) in enumerate(
            [(out_ref, out_hbm), (gate_ref, gate_hbm), (up_ref, up_hbm), (down_ref, down_hbm)]
        )
    ]
    tile = 256
    for at in range(0, width, tile):
        cols = pl.ds(at, tile)
        grads = dot(rows[:, cols], delta[...], 0, 0)
        gate_ref[cols] = grads[:, :units].astype(BF16)
        up_ref[cols] = grads[:, units:].astype(BF16)
    down_ref[...] = dot(hidden[...], rows[:, width:], 0, 0).astype(BF16)

    for copy in store[1:]:
        copy.start()

    for g in order:
        for p in pieces(g):
            r_copies[p].wait_recv()
    out_ref[...] = dot(spread, ret_in[...], 0, 0).astype(BF16)
    store[0].start()

    for g in range(n_groups):
        if g != late[0]:
            sent_group(g)
        for p in pieces(g):
            r_copies[p].wait_send()
        y_copies[g].wait_send()
        b_copies[g].wait_send()
    for copy in store:
        copy.wait()


def write_out(parts, *refs):
    ins, outs, held = refs[:4], refs[4:8], refs[8:12]
    in_sems, out_sems = refs[12:]
    loads, stores = [], []
    for i in range(4):
        size = ins[i].shape[0] // parts
        for j in range(parts):
            at = pl.ds(j * size, size)
            loads.append(pltpu.make_async_copy(ins[i].at[at], held[i].at[at], in_sems.at[i, j]))
            stores.append(pltpu.make_async_copy(held[i].at[at], outs[i].at[at], out_sems.at[i, j]))
    for load in loads:
        load.start()
    for load, store in zip(loads, stores):
        load.wait()
        store.start()
    for store in stores:
        store.wait()


def per_device(act_rows, cot_rows, expert_ids, w_gate, w_up, w_down):
    n_experts = lax.axis_size("expert")
    n_rows, width = act_rows.shape[1:]
    units = w_gate.shape[3]
    cap = 2 * n_rows // n_experts
    slots = n_experts * cap
    n_groups = slots // 32
    n_pieces = slots // min(cap, 32)
    dma = pltpu.SemaphoreType.DMA
    vmem = pl.BlockSpec(memory_space=pltpu.VMEM)
    hbm = pl.BlockSpec(memory_space=pltpu.HBM)
    shapes = (
        jax.ShapeDtypeStruct((n_rows, width), BF16),
        jax.ShapeDtypeStruct((width, units), BF16),
        jax.ShapeDtypeStruct((width, units), BF16),
        jax.ShapeDtypeStruct((units, width), BF16),
    )
    results = pl.pallas_call(
        functools.partial(kernel, n_experts, n_groups, cap),
        out_shape=shapes,
        in_specs=[hbm, hbm, vmem, hbm, hbm, hbm],
        out_specs=(hbm,) * 4,
        scratch_shapes=[
            pltpu.VMEM((n_rows, width), BF16),
            pltpu.VMEM((width, units), BF16),
            pltpu.VMEM((width, units), BF16),
            pltpu.VMEM((units, width), BF16),
            pltpu.VMEM((n_rows, width), BF16),
            pltpu.VMEM((n_rows, width), BF16),
            pltpu.VMEM((width, 2 * units), BF16),
            pltpu.VMEM((units, width), BF16),
            pltpu.VMEM((slots, 2 * width), BF16),
            pltpu.VMEM((2 * slots, 2 * width), BF16),
            pltpu.VMEM((2 * slots, 2 * units), BF16),
            pltpu.VMEM((2 * slots, units), BF16),
            pltpu.VMEM((slots, width), F32),
            pltpu.VMEM((slots, width), BF16),
            pltpu.VMEM((slots, width), BF16),
            pltpu.VMEM((slots, width), BF16),
            pltpu.VMEM((slots, width), BF16),
            dma((5,)),
            dma((4,)),
            dma((n_pieces,)),
            dma((n_pieces,)),
            dma((n_groups,)),
            dma((n_groups,)),
            dma((n_groups,)),
            dma((n_groups,)),
            dma((n_pieces,)),
            dma((n_pieces,)),
        ],
        compiler_params=pltpu.CompilerParams(
            collective_id=0, has_side_effects=True, vmem_limit_bytes=60 * 1024 * 1024
        ),
        cost_estimate=pl.CostEstimate(
            flops=32 * slots * width * units, bytes_accessed=9 * n_rows * width * 2, transcendentals=2 * slots * units
        ),
    )(act_rows[0], cot_rows[0], expert_ids.reshape(1, n_rows), w_gate[0, 0], w_up[0, 0], w_down[0, 0])
    outs = pl.pallas_call(
        functools.partial(write_out, 2),
        out_shape=shapes,
        in_specs=[hbm] * 4,
        out_specs=(hbm,) * 4,
        scratch_shapes=[pltpu.VMEM(shape.shape, shape.dtype) for shape in shapes] + [dma((4, 2)), dma((4, 2))],
        compiler_params=pltpu.CompilerParams(vmem_limit_bytes=60 * 1024 * 1024),
        cost_estimate=pl.CostEstimate(flops=0, bytes_accessed=16 * width * units, transcendentals=0),
    )(*results)
    return (outs[0][None], outs[1][None, None], outs[2][None, None], outs[3][None, None])


def solution(mesh):
    rows = P("section", "expert", None)
    weights = P("section", "expert", None, None)
    return jax.shard_map(
        per_device,
        mesh=mesh,
        in_specs=(rows, rows, rows, weights, weights, weights),
        out_specs=(rows, weights, weights, weights),
        check_vma=False,
    )
```

```python
import functools

import jax
import jax.numpy as jnp
from jax import lax
from jax.experimental import pallas as pl
from jax.experimental.pallas import tpu as pltpu
from jax.sharding import PartitionSpec as P

MESH = pl.DeviceIdType.MESH
F32 = jnp.float32
BF16 = jnp.bfloat16


def dot(a, b, a_dim, b_dim):
    return lax.dot_general(a, b, (((a_dim,), (b_dim,)), ((), ())), preferred_element_type=F32)


def partner_of(own, k, count):
    other = own
    bit = 1
    while bit < count:
        if k & bit:
            other = other + bit - 2 * bit * ((own // bit) % 2)
        bit *= 2
    return other


def kernel(
    n_experts, n_groups, cap,
    act_ref, cot_ref, ids_ref, wg_ref, wu_ref, wd_ref,
    out_hbm, gate_hbm, up_hbm, down_hbm,
    out_ref, gate_ref, up_ref, down_ref, act, cot, w_cat, wd, send, rows, delta, hidden, own_back, gate_up_sum, down_sum, mate_out, mate_in, ret_out, ret_in,
    loads, stores, zs, zr, ys, yr, bs, br, rs, rr,
):
    n_rows, width = act_ref.shape
    units = wg_ref.shape[1]
    slots = n_experts * cap
    group = slots // n_groups
    piece = min(cap, group)
    n_pieces = slots // piece
    per_group = n_pieces // n_groups
    half = lax.axis_size("section") // 2
    section = lax.axis_index("section")
    own = lax.axis_index("expert")
    mate = {"section": (section + half) % (2 * half)}
    partners = [{"expert": partner_of(own, k, n_experts)} for k in range(n_experts)]

    fetch = [
        pltpu.make_async_copy(src, dst, loads.at[i])
        for i, (src, dst) in enumerate(
            [
                (act_ref, act),
                (cot_ref, cot),
                (wg_ref, w_cat.at[:, pl.ds(0, units)]),
                (wu_ref, w_cat.at[:, pl.ds(units, units)]),
                (wd_ref, wd),
            ]
        )
    ]
    for copy in fetch:
        copy.start()

    barrier = pltpu.get_barrier_semaphore()
    for peer in partners[1:] + [mate]:
        pl.semaphore_signal(barrier, inc=1, device_id=peer, device_id_type=MESH)

    def remote(src, dst, send_sem, recv_sem, peer):
        return pltpu.make_async_remote_copy(
            src_ref=src, dst_ref=dst, send_sem=send_sem, recv_sem=recv_sem, device_id=peer, device_id_type=MESH
        )

    def peer_of(p):
        return p * piece // cap

    def piece_rows(p):
        return pl.ds(p * piece, piece)

    def rows_of(g, section_part=0):
        return pl.ds(section_part * slots + g * group, group)

    def pieces(g):
        return [p for p in range(g * per_group, (g + 1) * per_group) if peer_of(p) > 0]

    z_copies = [
        remote(send.at[piece_rows(p)], rows.at[piece_rows(p)], zs.at[p], zr.at[p], partners[peer_of(p)])
        if peer_of(p) > 0 else None
        for p in range(n_pieces)
    ]
    y_copies = [remote(rows.at[rows_of(g)], rows.at[rows_of(g, 1)], ys.at[g], yr.at[g], mate) for g in range(n_groups)]
    b_copies = [
        remote(mate_out.at[rows_of(g)], mate_in.at[rows_of(g)], bs.at[g], br.at[g], mate) for g in range(n_groups)
    ]
    r_copies = [
        remote(ret_out.at[piece_rows(p)], ret_in.at[piece_rows(p)], rs.at[p], rr.at[p], partners[peer_of(p)])
        if peer_of(p) > 0 else None
        for p in range(n_pieces)
    ]

    rel = ids_ref[...] ^ own
    kinds = -(-n_experts // 16) * 16
    onehot = (lax.broadcasted_iota(jnp.int32, (kinds, n_rows), 0) == rel).astype(F32)
    above = (
        lax.broadcasted_iota(jnp.int32, (n_rows, n_rows), 0) < lax.broadcasted_iota(jnp.int32, (n_rows, n_rows), 1)
    ).astype(F32)
    ranks = dot(onehot.astype(BF16), above.astype(BF16), 1, 0)
    place = rel * cap + jnp.sum(ranks * onehot, axis=0, keepdims=True).astype(jnp.int32)
    spread = (lax.broadcasted_iota(jnp.int32, (slots, n_rows), 0) == place).astype(F32).astype(BF16)

    for i, source in enumerate((act, cot)):
        fetch[i].wait()
        packed = dot(spread, source[...], 1, 0).astype(BF16)
        cols = pl.ds(i * width, width)
        send[cap:, cols] = packed[cap:]
        rows[:cap, cols] = packed[:cap]

    order = list(range(n_groups))
    if n_groups == 8:
        order = [0, 1, 2, 3, 6, 7, 4, 5]
    late = order[-2:]

    def send_group(g):
        for p in pieces(g):
            z_copies[p].start()

    def sent_group(g):
        for p in pieces(g):
            z_copies[p].wait_send()

    pl.semaphore_wait(barrier, n_experts)
    held_back = order[4:6] if n_groups == 8 and n_experts == 4 else []
    for g in order[:-2]:
        if g not in held_back:
            send_group(g)
    inner = ((own + 1) // 2) % 2 == 1

    if held_back:
        @pl.when(inner)
        def _():
            for g in held_back:
                send_group(g)

    def arrive(g):
        for p in pieces(g):
            z_copies[p].wait_recv()
        y_copies[g].start()

    def work(parts):
        acts = jnp.concatenate([rows[at, :width] for at in parts], axis=0)
        cots = jnp.concatenate([rows[at, width:] for at in parts], axis=0)
        pre = dot(acts, w_cat[...], 1, 0)
        gate_pre, up_pre = pre[:, :units], pre[:, units:]
        hidden_grad = dot(cots, wd[...], 1, 1)
        sigma = 1.0 / (1.0 + jnp.exp(-gate_pre))
        activ = gate_pre * sigma
        hid = (activ * up_pre).astype(BF16)
        gate_delta = (hidden_grad * up_pre * sigma * (1.0 + gate_pre * (1.0 - sigma))).astype(BF16)
        up_delta = (hidden_grad * activ).astype(BF16)
        both = jnp.concatenate([gate_delta, up_delta], axis=1)
        for i, at in enumerate(parts):
            hidden[at] = hid[i * group:(i + 1) * group]
            delta[at] = both[i * group:(i + 1) * group]
        back = dot(both, w_cat[...], 1, 1)
        return [back[i * group:(i + 1) * group] for i in range(len(parts))]

    def joint_work(own_group, mate_group):
        parts = []
        if mate_group is not None:
            y_copies[mate_group].wait_recv()
            parts.append(rows_of(mate_group, 1))
        if own_group is not None:
            parts.append(rows_of(own_group))
        back = work(parts)
        if mate_group is not None:
            mate_out[rows_of(mate_group)] = back[0].astype(BF16)
            b_copies[mate_group].start()
        if own_group is not None:
            own_back[rows_of(own_group)] = back[-1]

    def give_back(g):
        b_copies[g].wait_recv()
        total = (own_back[rows_of(g)] + mate_in[rows_of(g)].astype(F32)).astype(BF16)
        ret_out[rows_of(g)] = total
        for p in range(g * per_group, (g + 1) * per_group):
            if peer_of(p) > 0:
                r_copies[p].start()
            else:
                ret_in[piece_rows(p)] = total[(p - g * per_group) * piece:(p - g * per_group + 1) * piece]

    store = [
        pltpu.make_async_copy(src, dst, stores.at[i])
        for i, (src, dst) in enumerate(
            [(out_ref, out_hbm), (gate_ref, gate_hbm), (up_ref, up_hbm), (down_ref, down_hbm)]
        )
    ]
    tile = 256

    def runs(groups):
        found = []
        for g in sorted(groups):
            if found and found[-1][1] == g * group:
                found[-1][1] += group
            else:
                found.append([g * group, (g + 1) * group])
        return [pl.ds(part * slots + lo, hi - lo) for part in range(2) for lo, hi in found]

    def summed(pick, left, right):
        total = None
        for at in pick:
            term = dot(left(at), right(at), 0, 0)
            total = term if total is None else total + term
        return total

    def early_grads():
        pick = runs(order[:-2])
        for at in range(0, width, tile):
            cols = pl.ds(at, tile)
            gate_up_sum[cols] = summed(pick, lambda r: rows[r, cols], lambda r: delta[r])
        down_sum[...] = summed(pick, lambda r: hidden[r], lambda r: rows[r, width:])

    def final_grads():
        pick = runs(late)
        for at in range(0, width, tile):
            cols = pl.ds(at, tile)
            grads = gate_up_sum[cols] + summed(pick, lambda r: rows[r, cols], lambda r: delta[r])
            gate_ref[cols] = grads[:, :units].astype(BF16)
            up_ref[cols] = grads[:, units:].astype(BF16)
        down_ref[...] = (down_sum[...] + summed(pick, lambda r: hidden[r], lambda r: rows[r, width:])).astype(BF16)

    for i in range(n_groups + 3):
        if i < n_groups:
            arrive(order[i])
            if i == 3 and held_back:
                @pl.when(jnp.logical_not(inner))
                def _():
                    for g in held_back:
                        send_group(g)
            if i in (n_groups - 4, n_groups - 3):
                send_group(late[i - n_groups + 4])
            if i == 0:
                for copy in fetch[2:]:
                    copy.wait()
        if i <= n_groups:
            joint_work(order[i] if i < n_groups else None, order[i - 1] if i > 0 else None)
        if i >= 3:
            give_back(order[i - 3])
        if i == n_groups - 2:
            early_grads()

    final_grads()
    for copy in store[1:]:
        copy.start()

    for g in order:
        for p in pieces(g):
            r_copies[p].wait_recv()
    out_ref[...] = dot(spread, ret_in[...], 0, 0).astype(BF16)
    store[0].start()

    for g in range(n_groups):
        sent_group(g)
        for p in pieces(g):
            r_copies[p].wait_send()
        y_copies[g].wait_send()
        b_copies[g].wait_send()
    for copy in store:
        copy.wait()


def write_out(parts, *refs):
    ins, outs, held = refs[:4], refs[4:8], refs[8:12]
    in_sems, out_sems = refs[12:]
    loads, stores = [], []
    for i in range(4):
        size = ins[i].shape[0] // parts
        for j in range(parts):
            at = pl.ds(j * size, size)
            loads.append(pltpu.make_async_copy(ins[i].at[at], held[i].at[at], in_sems.at[i, j]))
            stores.append(pltpu.make_async_copy(held[i].at[at], outs[i].at[at], out_sems.at[i, j]))
    for load in loads:
        load.start()
    for load, store in zip(loads, stores):
        load.wait()
        store.start()
    for store in stores:
        store.wait()


def per_device(act_rows, cot_rows, expert_ids, w_gate, w_up, w_down):
    n_experts = lax.axis_size("expert")
    n_rows, width = act_rows.shape[1:]
    units = w_gate.shape[3]
    cap = 2 * n_rows // n_experts
    slots = n_experts * cap
    n_groups = slots // 32
    n_pieces = slots // min(cap, 32)
    dma = pltpu.SemaphoreType.DMA
    vmem = pl.BlockSpec(memory_space=pltpu.VMEM)
    hbm = pl.BlockSpec(memory_space=pltpu.HBM)
    shapes = (
        jax.ShapeDtypeStruct((n_rows, width), BF16),
        jax.ShapeDtypeStruct((width, units), BF16),
        jax.ShapeDtypeStruct((width, units), BF16),
        jax.ShapeDtypeStruct((units, width), BF16),
    )
    results = pl.pallas_call(
        functools.partial(kernel, n_experts, n_groups, cap),
        out_shape=shapes,
        in_specs=[hbm, hbm, vmem, hbm, hbm, hbm],
        out_specs=(hbm,) * 4,
        scratch_shapes=[
            pltpu.VMEM((n_rows, width), BF16),
            pltpu.VMEM((width, units), BF16),
            pltpu.VMEM((width, units), BF16),
            pltpu.VMEM((units, width), BF16),
            pltpu.VMEM((n_rows, width), BF16),
            pltpu.VMEM((n_rows, width), BF16),
            pltpu.VMEM((width, 2 * units), BF16),
            pltpu.VMEM((units, width), BF16),
            pltpu.VMEM((slots, 2 * width), BF16),
            pltpu.VMEM((2 * slots, 2 * width), BF16),
            pltpu.VMEM((2 * slots, 2 * units), BF16),
            pltpu.VMEM((2 * slots, units), BF16),
            pltpu.VMEM((slots, width), F32),
            pltpu.VMEM((width, 2 * units), F32),
            pltpu.VMEM((units, width), F32),
            pltpu.VMEM((slots, width), BF16),
            pltpu.VMEM((slots, width), BF16),
            pltpu.VMEM((slots, width), BF16),
            pltpu.VMEM((slots, width), BF16),
            dma((5,)),
            dma((4,)),
            dma((n_pieces,)),
            dma((n_pieces,)),
            dma((n_groups,)),
            dma((n_groups,)),
            dma((n_groups,)),
            dma((n_groups,)),
            dma((n_pieces,)),
            dma((n_pieces,)),
        ],
        compiler_params=pltpu.CompilerParams(
            collective_id=0, has_side_effects=True, vmem_limit_bytes=60 * 1024 * 1024
        ),
        cost_estimate=pl.CostEstimate(
            flops=32 * slots * width * units, bytes_accessed=9 * n_rows * width * 2, transcendentals=2 * slots * units
        ),
    )(act_rows[0], cot_rows[0], expert_ids.reshape(1, n_rows), w_gate[0, 0], w_up[0, 0], w_down[0, 0])
    outs = pl.pallas_call(
        functools.partial(write_out, 2),
        out_shape=shapes,
        in_specs=[hbm] * 4,
        out_specs=(hbm,) * 4,
        scratch_shapes=[pltpu.VMEM(shape.shape, shape.dtype) for shape in shapes] + [dma((4, 2)), dma((4, 2))],
        compiler_params=pltpu.CompilerParams(vmem_limit_bytes=60 * 1024 * 1024),
        cost_estimate=pl.CostEstimate(flops=0, bytes_accessed=16 * width * units, transcendentals=0),
    )(*results)
    return (outs[0][None], outs[1][None, None], outs[2][None, None], outs[3][None, None])


def solution(mesh):
    rows = P("section", "expert", None)
    weights = P("section", "expert", None, None)
    return jax.shard_map(
        per_device,
        mesh=mesh,
        in_specs=(rows, rows, rows, weights, weights, weights),
        out_specs=(rows, weights, weights, weights),
        check_vma=False,
    )
```

```python
import functools

import jax
import jax.numpy as jnp
from jax import lax
from jax.experimental import pallas as pl
from jax.experimental.pallas import tpu as pltpu
from jax.sharding import PartitionSpec as P

MESH = pl.DeviceIdType.MESH
F32 = jnp.float32
BF16 = jnp.bfloat16


def dot(a, b, a_dim, b_dim):
    return lax.dot_general(a, b, (((a_dim,), (b_dim,)), ((), ())), preferred_element_type=F32)


def partner_of(own, k, count):
    other = own
    bit = 1
    while bit < count:
        if k & bit:
            other = other + bit - 2 * bit * ((own // bit) % 2)
        bit *= 2
    return other


def kernel(
    n_experts, n_groups, cap,
    act_ref, cot_ref, ids_ref, wg_ref, wu_ref, wd_ref,
    out_hbm, gate_hbm, up_hbm, down_hbm,
    out_ref, gate_ref, up_ref, down_ref, act, cot, w_cat, wd, send, rows, delta, hidden, own_back, gate_up_sum, down_sum, mate_out, mate_in, ret_out, ret_in,
    loads, stores, zs, zr, ys, yr, bs, br, rs, rr,
):
    n_rows, width = act_ref.shape
    units = wg_ref.shape[1]
    slots = n_experts * cap
    group = slots // n_groups
    piece = min(cap, group)
    n_pieces = slots // piece
    per_group = n_pieces // n_groups
    half = lax.axis_size("section") // 2
    section = lax.axis_index("section")
    own = lax.axis_index("expert")
    mate = {"section": (section + half) % (2 * half)}
    partners = [{"expert": partner_of(own, k, n_experts)} for k in range(n_experts)]

    fetch = [
        pltpu.make_async_copy(src, dst, loads.at[i])
        for i, (src, dst) in enumerate(
            [
                (act_ref, act),
                (cot_ref, cot),
                (wg_ref, w_cat.at[:, pl.ds(0, units)]),
                (wu_ref, w_cat.at[:, pl.ds(units, units)]),
                (wd_ref, wd),
            ]
        )
    ]
    for copy in fetch:
        copy.start()

    barrier = pltpu.get_barrier_semaphore()
    for peer in partners[1:] + [mate]:
        pl.semaphore_signal(barrier, inc=1, device_id=peer, device_id_type=MESH)

    def remote(src, dst, send_sem, recv_sem, peer):
        return pltpu.make_async_remote_copy(
            src_ref=src, dst_ref=dst, send_sem=send_sem, recv_sem=recv_sem, device_id=peer, device_id_type=MESH
        )

    def peer_of(p):
        return p * piece // cap

    def piece_rows(p):
        return pl.ds(p * piece, piece)

    def rows_of(g, section_part=0):
        return pl.ds(section_part * slots + g * group, group)

    def pieces(g):
        return [p for p in range(g * per_group, (g + 1) * per_group) if peer_of(p) > 0]

    z_copies = [
        remote(send.at[piece_rows(p)], rows.at[piece_rows(p)], zs.at[p], zr.at[p], partners[peer_of(p)])
        if peer_of(p) > 0 else None
        for p in range(n_pieces)
    ]
    y_copies = [remote(rows.at[rows_of(g)], rows.at[rows_of(g, 1)], ys.at[g], yr.at[g], mate) for g in range(n_groups)]
    b_copies = [
        remote(mate_out.at[rows_of(g)], mate_in.at[rows_of(g)], bs.at[g], br.at[g], mate) for g in range(n_groups)
    ]
    r_copies = [
        remote(ret_out.at[piece_rows(p)], ret_in.at[piece_rows(p)], rs.at[p], rr.at[p], partners[peer_of(p)])
        if peer_of(p) > 0 else None
        for p in range(n_pieces)
    ]

    rel = ids_ref[...] ^ own
    kinds = -(-n_experts // 16) * 16
    onehot = (lax.broadcasted_iota(jnp.int32, (kinds, n_rows), 0) == rel).astype(F32)
    above = (
        lax.broadcasted_iota(jnp.int32, (n_rows, n_rows), 0) < lax.broadcasted_iota(jnp.int32, (n_rows, n_rows), 1)
    ).astype(F32)
    ranks = dot(onehot.astype(BF16), above.astype(BF16), 1, 0)
    place = rel * cap + jnp.sum(ranks * onehot, axis=0, keepdims=True).astype(jnp.int32)
    spread = (lax.broadcasted_iota(jnp.int32, (slots, n_rows), 0) == place).astype(F32).astype(BF16)

    for i, source in enumerate((act, cot)):
        fetch[i].wait()
        packed = dot(spread, source[...], 1, 0).astype(BF16)
        cols = pl.ds(i * width, width)
        send[cap:, cols] = packed[cap:]
        rows[:cap, cols] = packed[:cap]

    order = list(range(n_groups))
    if n_groups == 8:
        order = [0, 1, 2, 3, 6, 7, 4, 5]
    late = order[-2:]
    deferred = order[:2]

    def send_group(g):
        for p in pieces(g):
            z_copies[p].start()

    def sent_group(g):
        for p in pieces(g):
            z_copies[p].wait_send()

    pl.semaphore_wait(barrier, n_experts)
    held_back = order[4:6] if n_groups == 8 and n_experts == 4 else []
    for g in order[:-2]:
        if g not in held_back:
            send_group(g)
    inner = ((own + 1) // 2) % 2 == 1

    if held_back:
        @pl.when(inner)
        def _():
            for g in held_back:
                send_group(g)

    def arrive(g):
        for p in pieces(g):
            z_copies[p].wait_recv()
        y_copies[g].start()

    def work(parts):
        acts = jnp.concatenate([rows[at, :width] for at in parts], axis=0)
        cots = jnp.concatenate([rows[at, width:] for at in parts], axis=0)
        pre = dot(acts, w_cat[...], 1, 0)
        gate_pre, up_pre = pre[:, :units], pre[:, units:]
        hidden_grad = dot(cots, wd[...], 1, 1)
        sigma = 1.0 / (1.0 + jnp.exp(-gate_pre))
        activ = gate_pre * sigma
        hid = (activ * up_pre).astype(BF16)
        gate_delta = (hidden_grad * up_pre * sigma * (1.0 + gate_pre * (1.0 - sigma))).astype(BF16)
        up_delta = (hidden_grad * activ).astype(BF16)
        both = jnp.concatenate([gate_delta, up_delta], axis=1)
        for i, at in enumerate(parts):
            hidden[at] = hid[i * group:(i + 1) * group]
            delta[at] = both[i * group:(i + 1) * group]
        back = dot(both, w_cat[...], 1, 1)
        return [back[i * group:(i + 1) * group] for i in range(len(parts))]

    def joint_work(own_group, mate_group):
        parts = []
        if mate_group is not None:
            y_copies[mate_group].wait_recv()
            parts.append(rows_of(mate_group, 1))
        if own_group is not None:
            parts.append(rows_of(own_group))
        back = work(parts)
        if mate_group is not None:
            mate_out[rows_of(mate_group)] = back[0].astype(BF16)
            if mate_group not in deferred:
                b_copies[mate_group].start()
        if own_group is not None:
            own_back[rows_of(own_group)] = back[-1]

    def give_back(g):
        b_copies[g].wait_recv()
        total = (own_back[rows_of(g)] + mate_in[rows_of(g)].astype(F32)).astype(BF16)
        ret_out[rows_of(g)] = total
        for p in range(g * per_group, (g + 1) * per_group):
            if peer_of(p) > 0:
                r_copies[p].start()
            else:
                ret_in[piece_rows(p)] = total[(p - g * per_group) * piece:(p - g * per_group + 1) * piece]

    store = [
        pltpu.make_async_copy(src, dst, stores.at[i])
        for i, (src, dst) in enumerate(
            [(out_ref, out_hbm), (gate_ref, gate_hbm), (up_ref, up_hbm), (down_ref, down_hbm)]
        )
    ]
    tile = 256

    def runs(groups):
        found = []
        for g in sorted(groups):
            if found and found[-1][1] == g * group:
                found[-1][1] += group
            else:
                found.append([g * group, (g + 1) * group])
        return [pl.ds(part * slots + lo, hi - lo) for part in range(2) for lo, hi in found]

    def summed(pick, left, right):
        total = None
        for at in pick:
            term = dot(left(at), right(at), 0, 0)
            total = term if total is None else total + term
        return total

    def early_grads():
        pick = runs(order[:-2])
        for at in range(0, width, tile):
            cols = pl.ds(at, tile)
            gate_up_sum[cols] = summed(pick, lambda r: rows[r, cols], lambda r: delta[r])
        down_sum[...] = summed(pick, lambda r: hidden[r], lambda r: rows[r, width:])

    def final_grads():
        pick = runs(late)
        for at in range(0, width, tile):
            cols = pl.ds(at, tile)
            grads = gate_up_sum[cols] + summed(pick, lambda r: rows[r, cols], lambda r: delta[r])
            gate_ref[cols] = grads[:, :units].astype(BF16)
            up_ref[cols] = grads[:, units:].astype(BF16)
        down_ref[...] = (down_sum[...] + summed(pick, lambda r: hidden[r], lambda r: rows[r, width:])).astype(BF16)

    for i in range(n_groups + 3):
        if i < n_groups:
            arrive(order[i])
            if i == 3 and held_back:
                @pl.when(jnp.logical_not(inner))
                def _():
                    for g in held_back:
                        send_group(g)
            if i in (n_groups - 4, n_groups - 3):
                send_group(late[i - n_groups + 4])
            if i == 0:
                for copy in fetch[2:]:
                    copy.wait()
        if i <= n_groups:
            joint_work(order[i] if i < n_groups else None, order[i - 1] if i > 0 else None)
        if i == n_groups:
            b_copies[deferred[0]].start()
        if i >= 3 + len(deferred):
            give_back(order[i - 3])
        if i == n_groups - 2:
            early_grads()

    b_copies[deferred[1]].start()
    final_grads()
    for g in deferred:
        give_back(g)
    for copy in store[1:]:
        copy.start()

    for g in order:
        for p in pieces(g):
            r_copies[p].wait_recv()
    out_ref[...] = dot(spread, ret_in[...], 0, 0).astype(BF16)
    store[0].start()

    for g in range(n_groups):
        sent_group(g)
        for p in pieces(g):
            r_copies[p].wait_send()
        y_copies[g].wait_send()
        b_copies[g].wait_send()
    for copy in store:
        copy.wait()


def write_out(parts, *refs):
    ins, outs, held = refs[:4], refs[4:8], refs[8:12]
    in_sems, out_sems = refs[12:]
    loads, stores = [], []
    for i in range(4):
        size = ins[i].shape[0] // parts
        for j in range(parts):
            at = pl.ds(j * size, size)
            loads.append(pltpu.make_async_copy(ins[i].at[at], held[i].at[at], in_sems.at[i, j]))
            stores.append(pltpu.make_async_copy(held[i].at[at], outs[i].at[at], out_sems.at[i, j]))
    for load in loads:
        load.start()
    for load, store in zip(loads, stores):
        load.wait()
        store.start()
    for store in stores:
        store.wait()


def per_device(act_rows, cot_rows, expert_ids, w_gate, w_up, w_down):
    n_experts = lax.axis_size("expert")
    n_rows, width = act_rows.shape[1:]
    units = w_gate.shape[3]
    cap = 2 * n_rows // n_experts
    slots = n_experts * cap
    n_groups = slots // 32
    n_pieces = slots // min(cap, 32)
    dma = pltpu.SemaphoreType.DMA
    vmem = pl.BlockSpec(memory_space=pltpu.VMEM)
    hbm = pl.BlockSpec(memory_space=pltpu.HBM)
    shapes = (
        jax.ShapeDtypeStruct((n_rows, width), BF16),
        jax.ShapeDtypeStruct((width, units), BF16),
        jax.ShapeDtypeStruct((width, units), BF16),
        jax.ShapeDtypeStruct((units, width), BF16),
    )
    results = pl.pallas_call(
        functools.partial(kernel, n_experts, n_groups, cap),
        out_shape=shapes,
        in_specs=[hbm, hbm, vmem, hbm, hbm, hbm],
        out_specs=(hbm,) * 4,
        scratch_shapes=[
            pltpu.VMEM((n_rows, width), BF16),
            pltpu.VMEM((width, units), BF16),
            pltpu.VMEM((width, units), BF16),
            pltpu.VMEM((units, width), BF16),
            pltpu.VMEM((n_rows, width), BF16),
            pltpu.VMEM((n_rows, width), BF16),
            pltpu.VMEM((width, 2 * units), BF16),
            pltpu.VMEM((units, width), BF16),
            pltpu.VMEM((slots, 2 * width), BF16),
            pltpu.VMEM((2 * slots, 2 * width), BF16),
            pltpu.VMEM((2 * slots, 2 * units), BF16),
            pltpu.VMEM((2 * slots, units), BF16),
            pltpu.VMEM((slots, width), F32),
            pltpu.VMEM((width, 2 * units), F32),
            pltpu.VMEM((units, width), F32),
            pltpu.VMEM((slots, width), BF16),
            pltpu.VMEM((slots, width), BF16),
            pltpu.VMEM((slots, width), BF16),
            pltpu.VMEM((slots, width), BF16),
            dma((5,)),
            dma((4,)),
            dma((n_pieces,)),
            dma((n_pieces,)),
            dma((n_groups,)),
            dma((n_groups,)),
            dma((n_groups,)),
            dma((n_groups,)),
            dma((n_pieces,)),
            dma((n_pieces,)),
        ],
        compiler_params=pltpu.CompilerParams(
            collective_id=0, has_side_effects=True, vmem_limit_bytes=60 * 1024 * 1024
        ),
        cost_estimate=pl.CostEstimate(
            flops=32 * slots * width * units, bytes_accessed=9 * n_rows * width * 2, transcendentals=2 * slots * units
        ),
    )(act_rows[0], cot_rows[0], expert_ids.reshape(1, n_rows), w_gate[0, 0], w_up[0, 0], w_down[0, 0])
    outs = pl.pallas_call(
        functools.partial(write_out, 2),
        out_shape=shapes,
        in_specs=[hbm] * 4,
        out_specs=(hbm,) * 4,
        scratch_shapes=[pltpu.VMEM(shape.shape, shape.dtype) for shape in shapes] + [dma((4, 2)), dma((4, 2))],
        compiler_params=pltpu.CompilerParams(vmem_limit_bytes=60 * 1024 * 1024),
        cost_estimate=pl.CostEstimate(flops=0, bytes_accessed=16 * width * units, transcendentals=0),
    )(*results)
    return (outs[0][None], outs[1][None, None], outs[2][None, None], outs[3][None, None])


def solution(mesh):
    rows = P("section", "expert", None)
    weights = P("section", "expert", None, None)
    return jax.shard_map(
        per_device,
        mesh=mesh,
        in_specs=(rows, rows, rows, weights, weights, weights),
        out_specs=(rows, weights, weights, weights),
        check_vma=False,
    )
```

```python
import functools

import jax
import jax.numpy as jnp
from jax import lax
from jax.experimental import pallas as pl
from jax.experimental.pallas import tpu as pltpu
from jax.sharding import PartitionSpec as P

MESH = pl.DeviceIdType.MESH
F32 = jnp.float32
BF16 = jnp.bfloat16


def dot(a, b, a_dim, b_dim):
    return lax.dot_general(a, b, (((a_dim,), (b_dim,)), ((), ())), preferred_element_type=F32)


def partner_of(own, k, count):
    other = own
    bit = 1
    while bit < count:
        if k & bit:
            other = other + bit - 2 * bit * ((own // bit) % 2)
        bit *= 2
    return other


def kernel(
    n_experts, n_groups, cap,
    act_ref, cot_ref, ids_ref, wg_ref, wu_ref, wd_ref,
    out_hbm, gate_hbm, up_hbm, down_hbm,
    out_ref, gate_ref, up_ref, down_ref, act, cot, w_cat, wd, send, rows, delta, hidden, own_back, gate_up_sum, down_sum, mate_out, mate_in, ret_out, ret_in,
    loads, stores, zs, zr, ys, yr, bs, br, rs, rr,
):
    n_rows, width = act_ref.shape
    units = wg_ref.shape[1]
    slots = n_experts * cap
    group = slots // n_groups
    piece = min(cap, group)
    n_pieces = slots // piece
    per_group = n_pieces // n_groups
    half = lax.axis_size("section") // 2
    section = lax.axis_index("section")
    own = lax.axis_index("expert")
    mate = {"section": (section + half) % (2 * half)}
    partners = [{"expert": partner_of(own, k, n_experts)} for k in range(n_experts)]

    fetch = [
        pltpu.make_async_copy(src, dst, loads.at[i])
        for i, (src, dst) in enumerate(
            [
                (act_ref, act),
                (cot_ref, cot),
                (wg_ref, w_cat.at[:, pl.ds(0, units)]),
                (wu_ref, w_cat.at[:, pl.ds(units, units)]),
                (wd_ref, wd),
            ]
        )
    ]
    for copy in fetch:
        copy.start()

    barrier = pltpu.get_barrier_semaphore()
    for peer in partners[1:] + [mate]:
        pl.semaphore_signal(barrier, inc=1, device_id=peer, device_id_type=MESH)

    def remote(src, dst, send_sem, recv_sem, peer):
        return pltpu.make_async_remote_copy(
            src_ref=src, dst_ref=dst, send_sem=send_sem, recv_sem=recv_sem, device_id=peer, device_id_type=MESH
        )

    def peer_of(p):
        return p * piece // cap

    def piece_rows(p):
        return pl.ds(p * piece, piece)

    def rows_of(g, section_part=0):
        return pl.ds(section_part * slots + g * group, group)

    def pieces(g):
        return [p for p in range(g * per_group, (g + 1) * per_group) if peer_of(p) > 0]

    z_copies = [
        remote(send.at[piece_rows(p)], rows.at[piece_rows(p)], zs.at[p], zr.at[p], partners[peer_of(p)])
        if peer_of(p) > 0 else None
        for p in range(n_pieces)
    ]
    y_copies = [remote(rows.at[rows_of(g)], rows.at[rows_of(g, 1)], ys.at[g], yr.at[g], mate) for g in range(n_groups)]
    b_copies = [
        remote(mate_out.at[rows_of(g)], mate_in.at[rows_of(g)], bs.at[g], br.at[g], mate) for g in range(n_groups)
    ]
    r_copies = [
        remote(ret_out.at[piece_rows(p)], ret_in.at[piece_rows(p)], rs.at[p], rr.at[p], partners[peer_of(p)])
        if peer_of(p) > 0 else None
        for p in range(n_pieces)
    ]

    rel = ids_ref[...] ^ own
    kinds = -(-n_experts // 16) * 16
    onehot = (lax.broadcasted_iota(jnp.int32, (kinds, n_rows), 0) == rel).astype(F32)
    above = (
        lax.broadcasted_iota(jnp.int32, (n_rows, n_rows), 0) < lax.broadcasted_iota(jnp.int32, (n_rows, n_rows), 1)
    ).astype(F32)
    ranks = dot(onehot.astype(BF16), above.astype(BF16), 1, 0)
    place = rel * cap + jnp.sum(ranks * onehot, axis=0, keepdims=True).astype(jnp.int32)
    spread = (lax.broadcasted_iota(jnp.int32, (slots, n_rows), 0) == place).astype(F32).astype(BF16)

    for i, source in enumerate((act, cot)):
        fetch[i].wait()
        rows[:cap, pl.ds(i * width, width)] = dot(spread[:cap], source[...], 1, 0).astype(BF16)
    pl.semaphore_wait(barrier, n_experts)
    ready = [g for g in range(n_groups) if not pieces(g)]
    for g in ready:
        y_copies[g].start()
    for i, source in enumerate((act, cot)):
        send[cap:, pl.ds(i * width, width)] = dot(spread[cap:], source[...], 1, 0).astype(BF16)

    order = list(range(n_groups))
    if n_groups == 8:
        order = [0, 1, 2, 3, 6, 7, 4, 5]
    late = order[-2:]
    deferred = order[:2]

    def send_group(g):
        for p in pieces(g):
            z_copies[p].start()

    def sent_group(g):
        for p in pieces(g):
            z_copies[p].wait_send()

    held_back = order[4:6] if n_groups == 8 and n_experts == 4 else []
    for g in order[:-2]:
        if g not in held_back:
            send_group(g)
    inner = ((own + 1) // 2) % 2 == 1

    if held_back:
        @pl.when(inner)
        def _():
            for g in held_back:
                send_group(g)

    def arrive(g):
        for p in pieces(g):
            z_copies[p].wait_recv()
        if g not in ready:
            y_copies[g].start()

    def work(parts):
        acts = jnp.concatenate([rows[at, :width] for at in parts], axis=0)
        cots = jnp.concatenate([rows[at, width:] for at in parts], axis=0)
        pre = dot(acts, w_cat[...], 1, 0)
        gate_pre, up_pre = pre[:, :units], pre[:, units:]
        hidden_grad = dot(cots, wd[...], 1, 1)
        sigma = 1.0 / (1.0 + jnp.exp(-gate_pre))
        activ = gate_pre * sigma
        hid = (activ * up_pre).astype(BF16)
        gate_delta = (hidden_grad * up_pre * sigma * (1.0 + gate_pre * (1.0 - sigma))).astype(BF16)
        up_delta = (hidden_grad * activ).astype(BF16)
        both = jnp.concatenate([gate_delta, up_delta], axis=1)
        for i, at in enumerate(parts):
            hidden[at] = hid[i * group:(i + 1) * group]
            delta[at] = both[i * group:(i + 1) * group]
        back = dot(both, w_cat[...], 1, 1)
        return [back[i * group:(i + 1) * group] for i in range(len(parts))]

    def joint_work(own_group, mate_group):
        parts = []
        if mate_group is not None:
            y_copies[mate_group].wait_recv()
            parts.append(rows_of(mate_group, 1))
        if own_group is not None:
            parts.append(rows_of(own_group))
        back = work(parts)
        if mate_group is not None:
            mate_out[rows_of(mate_group)] = back[0].astype(BF16)
            if mate_group not in deferred:
                b_copies[mate_group].start()
        if own_group is not None:
            own_back[rows_of(own_group)] = back[-1]

    def give_back(g):
        b_copies[g].wait_recv()
        total = (own_back[rows_of(g)] + mate_in[rows_of(g)].astype(F32)).astype(BF16)
        ret_out[rows_of(g)] = total
        for p in range(g * per_group, (g + 1) * per_group):
            if peer_of(p) > 0:
                r_copies[p].start()
            else:
                ret_in[piece_rows(p)] = total[(p - g * per_group) * piece:(p - g * per_group + 1) * piece]

    store = [
        pltpu.make_async_copy(src, dst, stores.at[i])
        for i, (src, dst) in enumerate(
            [(out_ref, out_hbm), (gate_ref, gate_hbm), (up_ref, up_hbm), (down_ref, down_hbm)]
        )
    ]
    tile = 256

    def runs(groups):
        found = []
        for g in sorted(groups):
            if found and found[-1][1] == g * group:
                found[-1][1] += group
            else:
                found.append([g * group, (g + 1) * group])
        return [pl.ds(part * slots + lo, hi - lo) for part in range(2) for lo, hi in found]

    def summed(pick, left, right):
        total = None
        for at in pick:
            term = dot(left(at), right(at), 0, 0)
            total = term if total is None else total + term
        return total

    def early_grads():
        pick = runs(order[:-2])
        for at in range(0, width, tile):
            cols = pl.ds(at, tile)
            gate_up_sum[cols] = summed(pick, lambda r: rows[r, cols], lambda r: delta[r])
        down_sum[...] = summed(pick, lambda r: hidden[r], lambda r: rows[r, width:])

    def final_grads():
        pick = runs(late)
        for at in range(0, width, tile):
            cols = pl.ds(at, tile)
            grads = gate_up_sum[cols] + summed(pick, lambda r: rows[r, cols], lambda r: delta[r])
            gate_ref[cols] = grads[:, :units].astype(BF16)
            up_ref[cols] = grads[:, units:].astype(BF16)
        down_ref[...] = (down_sum[...] + summed(pick, lambda r: hidden[r], lambda r: rows[r, width:])).astype(BF16)

    for i in range(n_groups + 3):
        if i < n_groups:
            arrive(order[i])
            if i == 3 and held_back:
                @pl.when(jnp.logical_not(inner))
                def _():
                    for g in held_back:
                        send_group(g)
            if i in (n_groups - 4, n_groups - 3):
                send_group(late[i - n_groups + 4])
            if i == 0:
                for copy in fetch[2:]:
                    copy.wait()
        if i <= n_groups:
            joint_work(order[i] if i < n_groups else None, order[i - 1] if i > 0 else None)
        if i == n_groups:
            b_copies[deferred[0]].start()
        if i >= 3 + len(deferred):
            give_back(order[i - 3])
        if i == n_groups - 2:
            early_grads()

    b_copies[deferred[1]].start()
    final_grads()
    for g in deferred:
        give_back(g)
    for copy in store[1:]:
        copy.start()

    for g in order:
        for p in pieces(g):
            r_copies[p].wait_recv()
    out_ref[...] = dot(spread, ret_in[...], 0, 0).astype(BF16)
    store[0].start()

    for g in range(n_groups):
        sent_group(g)
        for p in pieces(g):
            r_copies[p].wait_send()
        y_copies[g].wait_send()
        b_copies[g].wait_send()
    for copy in store:
        copy.wait()


def write_out(parts, *refs):
    ins, outs, held = refs[:4], refs[4:8], refs[8:12]
    in_sems, out_sems = refs[12:]
    loads, stores = [], []
    for i in range(4):
        size = ins[i].shape[0] // parts
        for j in range(parts):
            at = pl.ds(j * size, size)
            loads.append(pltpu.make_async_copy(ins[i].at[at], held[i].at[at], in_sems.at[i, j]))
            stores.append(pltpu.make_async_copy(held[i].at[at], outs[i].at[at], out_sems.at[i, j]))
    for load in loads:
        load.start()
    for load, store in zip(loads, stores):
        load.wait()
        store.start()
    for store in stores:
        store.wait()


def per_device(act_rows, cot_rows, expert_ids, w_gate, w_up, w_down):
    n_experts = lax.axis_size("expert")
    n_rows, width = act_rows.shape[1:]
    units = w_gate.shape[3]
    cap = 2 * n_rows // n_experts
    slots = n_experts * cap
    n_groups = slots // 32
    n_pieces = slots // min(cap, 32)
    dma = pltpu.SemaphoreType.DMA
    vmem = pl.BlockSpec(memory_space=pltpu.VMEM)
    hbm = pl.BlockSpec(memory_space=pltpu.HBM)
    shapes = (
        jax.ShapeDtypeStruct((n_rows, width), BF16),
        jax.ShapeDtypeStruct((width, units), BF16),
        jax.ShapeDtypeStruct((width, units), BF16),
        jax.ShapeDtypeStruct((units, width), BF16),
    )
    results = pl.pallas_call(
        functools.partial(kernel, n_experts, n_groups, cap),
        out_shape=shapes,
        in_specs=[hbm, hbm, vmem, hbm, hbm, hbm],
        out_specs=(hbm,) * 4,
        scratch_shapes=[
            pltpu.VMEM((n_rows, width), BF16),
            pltpu.VMEM((width, units), BF16),
            pltpu.VMEM((width, units), BF16),
            pltpu.VMEM((units, width), BF16),
            pltpu.VMEM((n_rows, width), BF16),
            pltpu.VMEM((n_rows, width), BF16),
            pltpu.VMEM((width, 2 * units), BF16),
            pltpu.VMEM((units, width), BF16),
            pltpu.VMEM((slots, 2 * width), BF16),
            pltpu.VMEM((2 * slots, 2 * width), BF16),
            pltpu.VMEM((2 * slots, 2 * units), BF16),
            pltpu.VMEM((2 * slots, units), BF16),
            pltpu.VMEM((slots, width), F32),
            pltpu.VMEM((width, 2 * units), F32),
            pltpu.VMEM((units, width), F32),
            pltpu.VMEM((slots, width), BF16),
            pltpu.VMEM((slots, width), BF16),
            pltpu.VMEM((slots, width), BF16),
            pltpu.VMEM((slots, width), BF16),
            dma((5,)),
            dma((4,)),
            dma((n_pieces,)),
            dma((n_pieces,)),
            dma((n_groups,)),
            dma((n_groups,)),
            dma((n_groups,)),
            dma((n_groups,)),
            dma((n_pieces,)),
            dma((n_pieces,)),
        ],
        compiler_params=pltpu.CompilerParams(
            collective_id=0, has_side_effects=True, vmem_limit_bytes=60 * 1024 * 1024
        ),
        cost_estimate=pl.CostEstimate(
            flops=32 * slots * width * units, bytes_accessed=9 * n_rows * width * 2, transcendentals=2 * slots * units
        ),
    )(act_rows[0], cot_rows[0], expert_ids.reshape(1, n_rows), w_gate[0, 0], w_up[0, 0], w_down[0, 0])
    outs = pl.pallas_call(
        functools.partial(write_out, 2),
        out_shape=shapes,
        in_specs=[hbm] * 4,
        out_specs=(hbm,) * 4,
        scratch_shapes=[pltpu.VMEM(shape.shape, shape.dtype) for shape in shapes] + [dma((4, 2)), dma((4, 2))],
        compiler_params=pltpu.CompilerParams(vmem_limit_bytes=60 * 1024 * 1024),
        cost_estimate=pl.CostEstimate(flops=0, bytes_accessed=16 * width * units, transcendentals=0),
    )(*results)
    return (outs[0][None], outs[1][None, None], outs[2][None, None], outs[3][None, None])


def solution(mesh):
    rows = P("section", "expert", None)
    weights = P("section", "expert", None, None)
    return jax.shard_map(
        per_device,
        mesh=mesh,
        in_specs=(rows, rows, rows, weights, weights, weights),
        out_specs=(rows, weights, weights, weights),
        check_vma=False,
    )
```
